256 devices in a mesh: dp: 32 (over y, z), tensor: 8 (over x, core).
Axes of the slice: x: 4, y: 4, z: 8, core: 2. Of those that a mesh axis runs over, the one named last changes fastest.
Arguments:
- context: bfloat16 [16384, 2048], P('dp', 'tensor'), may hold values from -6 to 6
- cotangent: bfloat16 [16384, 4096], P(('dp', 'tensor')), may hold values from -1.2 to 1.2
- row_order: int32 [32, 512], P('dp'), may hold values from 0 to 511, each once within a row
- out_weight: bfloat16 [2048, 4096], P('tensor'), may hold values from -0.125 to 0.125
Outputs:
- weight_grad: float32 [2048, 4096], P('tensor', 'dp')
- context_grad: bfloat16 [16384, 2048], P('dp', 'tensor')
The draws below stay inside these ranges and needn't reach their ends.
Inputs may be any that keep to these rules, and one draw needn't show every extreme that they name: Each row of row_order is a permutation of 0 to 511.
All inputs are finite; a program needn't handle non-finite values.
Results may differ from the reference program's by a relative error of at most 0.0045.
Values may be sent and summed in bfloat16 or wider, within the bound.
A program may use at most 64 MiB of HBM per device.

```python
import jax
import jax.numpy as jnp
import numpy as np
from jax import lax

D = 4096
HK = 2048
RG = 512
ROWS = 16384
LEVELS = 5
N_DP = 32


def draw_context(key, part):
    key = jax.random.fold_in(key, 11)
    key_mean, key_noise, key_gain = jax.random.split(key, 3)
    mean = 0.2 * jnp.clip(jax.random.normal(key_mean, (HK,), jnp.float32), -4.0, 4.0)
    gains = jnp.exp(jax.random.uniform(key_gain, (ROWS // RG,), jnp.float32, -0.7, 0.0))
    noise = jnp.clip(jax.random.normal(key_noise, (ROWS, HK), jnp.float32), -4.0, 4.0)
    values = (noise + mean[None, :]).reshape(ROWS // RG, RG, HK) * gains[:, None, None]
    return values.reshape(ROWS, HK).astype(jnp.bfloat16)


def draw_cotangent(key, part):
    key = jax.random.fold_in(key, 23)
    key_mean, key_noise, key_gain = jax.random.split(key, 3)
    mean = 0.04 * jnp.clip(jax.random.normal(key_mean, (D,), jnp.float32), -4.0, 4.0)
    gains = jnp.exp(jax.random.uniform(key_gain, (ROWS // RG,), jnp.float32, -1.0, 0.0))
    noise = 0.2 * jnp.clip(jax.random.normal(key_noise, (ROWS, D), jnp.float32), -4.0, 4.0)
    values = (noise + mean[None, :]).reshape(ROWS // RG, RG, D) * gains[:, None, None]
    return values.reshape(ROWS, D).astype(jnp.bfloat16)


def block_levels(key, extent, shards, low, top_value):
    def one(position, shards_of):
        draws = jax.random.uniform(jax.random.fold_in(jax.random.fold_in(key, 6), position), (shards_of,), jnp.float32, low / len(shards), top_value / len(shards))
        return jnp.repeat(jnp.exp(draws), extent[position] // shards_of).reshape((-1,) + (1,) * (len(extent) - position - 1))

    gain = one(*shards[0])
    for cut in shards[1:]:
        gain = gain * one(*cut)
    return gain


def bell_draw(key, shape, scale, bound, cuts=(), kind=jnp.bfloat16):
    factor_of = block_levels(key, shape, cuts, -0.22, 0.18) if cuts else 1.0
    values = jax.random.normal(key, shape, jnp.float32) * scale * factor_of
    return jnp.minimum(jnp.maximum(values, -bound), bound).astype(kind)


def setup_inputs(seed: int = 0) -> dict:
    arg_keys = jax.random.split(jax.random.key(seed), 5)
    context = draw_context(jax.random.fold_in(arg_keys[4], 71), 0)
    cotangent = draw_cotangent(jax.random.fold_in(arg_keys[4], 71), 0)
    row_order = jax.vmap(lambda own: jax.random.permutation(own, RG))(jax.random.split(arg_keys[2], N_DP)).reshape((N_DP, RG)).astype(jnp.int32)
    out_weight = bell_draw(arg_keys[3], (HK, D), HK ** -0.5, 0.125, ((0, 8),))
    return dict(context=context, cotangent=cotangent, row_order=row_order, out_weight=out_weight)


EPS = 1e-6


def reference(context, cotangent, row_order, out_weight):
    blocks = cotangent.reshape(N_DP, RG, D)
    used = jnp.take_along_axis(blocks, row_order[:, :, None].astype(jnp.int32), axis=1)
    ctx_blocks = context.reshape(N_DP, RG, HK)

    def per_block(pair):
        ctx_rows, cot_rows = pair
        grad_one = jnp.dot(ctx_rows.T, cot_rows, preferred_element_type=jnp.float32)
        back = jnp.dot(cot_rows, out_weight.T, preferred_element_type=jnp.float32).astype(jnp.bfloat16)
        return grad_one, back

    grads, backs = lax.map(per_block, (ctx_blocks, used))
    for level in range(LEVELS):
        partner = grads[np.arange(N_DP) ^ (1 << level)]
        s_ab = jnp.sum(grads * partner, axis=(1, 2))
        s_aa = jnp.sum(grads * grads, axis=(1, 2))
        s_bb = jnp.sum(partner * partner, axis=(1, 2))
        left = 1.0 - s_ab / (2.0 * (s_aa + EPS))
        right = 1.0 - s_ab / (2.0 * (s_bb + EPS))
        grads = left[:, None, None] * grads + right[:, None, None] * partner
    return grads[0], backs.reshape(ROWS, HK)
```

```python
import jax
import jax.numpy as jnp
from jax import lax
from jax.experimental import pallas as pl
from jax.experimental.pallas import tpu as pltpu
from jax.sharding import PartitionSpec as P

EPS = 1e-06
MESH = pl.DeviceIdType.MESH
BF16, F32 = jnp.bfloat16, jnp.float32
NY, NZ, NX, NC = 4, 8, 4, 2
ROWS, SHARD = 512, 64
HEADS, D = 256, 4096
SLICE = D // NZ
WIDE = D // (NY * NZ)
HALF = HEADS // 2
N_DP = NY * NZ
PEERS_A = [(dz, dc) for dz in (4, 3, 5, 2, 6, 1, 7, 0) for dc in (1, 0) if dz or dc]
PEERS_B = [(dy, dx) for dy, dx in sorted(((a, b) for a in range(NY) for b in range(NX)), key=lambda p: -min(p[0], NY - p[0]) - min(p[1], NX - p[1])) if dy or dx]
ORDER = (0, 1, 7, 2, 6, 3, 5, 4)


def kernel(
    context, cotangent, row_order, out_weight, out_grad, out_back,
    uf, us, pack, ct, cv, ov, wv, pt, gst, gv, acc, src_a, src_b, in_a, in_b, wts,
    local, us_s, us_r, aa_s, aa_r, uf_s, uf_r, ct_s, ct_r, gv_s, gv_r, a_s, a_r, b_s, b_r,
):
    dp, tp = lax.axis_index("dp"), lax.axis_index("tensor")
    y, z = lax.div(dp, NZ), lax.rem(dp, NZ)
    x, c = lax.div(tp, NC), lax.rem(tp, NC)

    def device(dy=0, dz=0, dx=0, dc=0):
        return (
            lax.rem(y + dy, NY) * NZ + lax.rem(z + dz, NZ),
            lax.rem(x + dx, NX) * NC + lax.rem(c + dc, NC),
        )

    started = []

    def send(source, target, send_sem, recv_sem, where):
        copy = pltpu.make_async_remote_copy(
            src_ref=source, dst_ref=target, send_sem=send_sem, recv_sem=recv_sem,
            device_id=where, device_id_type=MESH,
        )
        copy.start()
        started.append(copy)
        return copy

    barrier = pltpu.get_barrier_semaphore()
    for dz, dc in PEERS_A:
        pl.semaphore_signal(barrier, inc=1, device_id=device(dz=dz, dc=dc), device_id_type=MESH)
    for dy, dx in PEERS_B:
        pl.semaphore_signal(barrier, inc=1, device_id=device(dy=dy, dx=dx), device_id_type=MESH)

    load_cot = pltpu.make_async_copy(cotangent, uf.at[c, x], local.at[0])
    load_ctx = pltpu.make_async_copy(context, cv, local.at[1])
    load_ord = pltpu.make_async_copy(row_order, ov, local.at[2])
    load_w = pltpu.make_async_copy(out_weight, wv, local.at[3])
    load_cot.start()
    load_ctx.start()
    load_ord.start()
    load_w.start()

    load_cot.wait()
    for d in range(NZ):
        to = lax.rem(z + d, NZ)
        for j in range(NY):
            at = pl.multiple_of((j * NZ + to) * WIDE, WIDE)
            block = uf[c, x, :, pl.ds(at, WIDE)]
            if d == 0:
                us[0, c, x, :, j * WIDE : (j + 1) * WIDE] = block
            else:
                pack[d - 1, :, j * WIDE : (j + 1) * WIDE] = block
    pl.semaphore_wait(barrier, len(PEERS_A) + len(PEERS_B))

    right, left, sibling = device(dx=1), device(dx=NX - 1), device(dc=1)
    xl, xr, xf = lax.rem(x + NX - 1, NX), lax.rem(x + 1, NX), lax.rem(x + 2, NX)
    lo, hi = pl.ds(0, SHARD // 2), pl.ds(SHARD // 2, SHARD // 2)
    copies = {}

    def us_own(d):
        mine = us.at[d, c, x]
        copies["us", d, 0] = send(mine, mine, us_s.at[d, 0], us_r.at[d, 0], right)
        copies["us", d, 1] = send(mine, mine, us_s.at[d, 1], us_r.at[d, 1], left)

    def us_forward(d):
        copies["us", d, 0].wait_recv()
        part = us.at[d, c, xl, lo]
        copies["us", d, 2] = send(part, part, us_s.at[d, 2], us_r.at[d, 2], right)
        copies["us", d, 1].wait_recv()
        part = us.at[d, c, xr, hi]
        copies["us", d, 3] = send(part, part, us_s.at[d, 3], us_r.at[d, 3], left)

    def us_share(d):
        copies["us", d, 2].wait_recv()
        copies["us", d, 3].wait_recv()
        part = us.at[d, c]
        copies["us", d, 4] = send(part, part, us_s.at[d, 4], us_r.at[d, 4], sibling)

    def uf_own():
        for k, (rows, to) in enumerate(((lo, right), (hi, left), (hi, right), (lo, left))):
            part = uf.at[c, x, rows]
            copies["uf", k] = send(part, part, uf_s.at[k], uf_r.at[k], to)
        part = uf.at[c, x]
        copies["uf", 6] = send(part, part, uf_s.at[6], uf_r.at[6], sibling)

    def uf_forward():
        copies["uf", 0].wait_recv()
        part = uf.at[c, xl, lo]
        copies["uf", 4] = send(part, part, uf_s.at[4], uf_r.at[4], right)
        copies["uf", 1].wait_recv()
        part = uf.at[c, xr, hi]
        copies["uf", 5] = send(part, part, uf_s.at[5], uf_r.at[5], left)

    def uf_share():
        copies["uf", 2].wait_recv()
        part = uf.at[c, xl]
        copies["uf", 7] = send(part, part, uf_s.at[7], uf_r.at[7], sibling)
        copies["uf", 3].wait_recv()
        part = uf.at[c, xr]
        copies["uf", 8] = send(part, part, uf_s.at[8], uf_r.at[8], sibling)
        copies["uf", 4].wait_recv()
        copies["uf", 5].wait_recv()
        part = uf.at[c, xf]
        copies["uf", 9] = send(part, part, uf_s.at[9], uf_r.at[9], sibling)

    def ct_send(slot, h, step):
        to = (slot - step) % NZ
        copies["ct", to, h] = send(
            ct.at[slot, h], ct.at[to, h], ct_s.at[to, h], ct_r.at[to, h], device(dz=step % NZ)
        )

    def ct_arrived(d):
        for h in range(2):
            copies["ct", d, h].wait_recv()
            if d in (7, 6) or (d == 5 and h == 0):
                ct_send(d, h, 1)
            if d in (1, 2) or (d == 3 and h == 1):
                ct_send(d, h, -1)

    def replica(d, e=0):
        return lax.rem(y + e, NY) * NZ + lax.rem(z + d, NZ)

    def gradient(d, h):
        value = jnp.dot(ct[d, h], us[d].reshape(ROWS, SLICE), preferred_element_type=F32).astype(BF16)
        for j in range(NY):
            gst[d, h, j] = value[:, j * WIDE : (j + 1) * WIDE]
        b = replica(d)
        target = gv.at[b, pl.ds(h * HALF, HALF)]
        for e in (2, 1, 3):
            copies["gv", d, h, e] = send(
                gst.at[d, h, lax.rem(y + e, NY)], target, gv_s.at[d, h, e - 1], gv_r.at[d, h, e - 1], device(dy=e)
            )
        gv[b, h * HALF : (h + 1) * HALF] = gst[d, h, y]

    def gram_pair(d1, d2):
        first = [replica(d1, e) for e in range(NY)]
        second = [replica(d2, e) for e in range(NY)]
        pairs = [(i, j) for i in range(NY) for j in range(NY) if d1 != d2 or i <= j]

        def body(step, sums):
            at = pl.ds(pl.multiple_of(step * 16, 16), 16)
            a = [gv[b, at].astype(F32) for b in first]
            bs = a if d1 == d2 else [gv[b, at].astype(F32) for b in second]
            return tuple(s + a[i] * bs[j] for s, (i, j) in zip(sums, pairs))

        sums = lax.fori_loop(0, HEADS // 16, body, tuple(jnp.zeros((16, WIDE), F32) for _ in pairs))
        for s, (i, j) in zip(sums, pairs):
            line = jnp.sum(s, axis=0, keepdims=True)
            zi, yi = lax.rem(z + d1, NZ), lax.rem(y + i, NY)
            zj, yj = lax.rem(z + d2, NZ), lax.rem(y + j, NY)
            acc[pl.ds(zi * 128 + yi * N_DP + yj * NZ + zj, 1), :] = line
            acc[pl.ds(zj * 128 + yj * N_DP + yi * NZ + zi, 1), :] = line

    done = []

    def gram(d):
        for h in range(2):
            for e in (1, 3, 2):
                copies["gv", d, h, e].wait_recv()
        done.append(d)
        for other in done:
            gram_pair(d, other)

    us_own(0)
    for d in ORDER[1:]:
        copies["aa", NZ - d] = send(
            pack.at[d - 1], us.at[NZ - d, c, x], aa_s.at[NZ - d], aa_r.at[NZ - d], device(dz=d)
        )

    load_ctx.wait()
    load_ord.wait()
    row = lax.broadcasted_iota(jnp.int32, (ROWS, ROWS), 0)
    name = lax.rem(lax.div(row, SHARD), NX) * (NC * SHARD) + lax.div(row, NX * SHARD) * SHARD + lax.rem(row, SHARD)
    pt[...] = (ov[...] == name).astype(F32).astype(BF16)
    mine = lax.dot_general(cv[...], pt[...], (((0,), (1,)), ((), ())), preferred_element_type=F32).astype(BF16)
    ct[0, 0] = mine[:HALF]
    ct[0, 1] = mine[HALF:]
    for h in range(2):
        ct_send(0, h, 1)
        ct_send(0, h, -1)

    us_forward(0)
    for d in (1, 7):
        copies["aa", d].wait_recv()
        us_own(d)
    us_share(0)
    for d in (1, 7):
        us_forward(d)
    for d in (2, 6):
        copies["aa", d].wait_recv()
        us_own(d)
    copies["us", 0, 4].wait_recv()
    gradient(0, 0)
    gradient(0, 1)
    for d in (1, 7):
        us_share(d)
    ct_arrived(7)
    ct_arrived(1)
    for d in (2, 6):
        us_forward(d)
    for d in (3, 5, 4):
        copies["aa", d].wait_recv()
        us_own(d)
    for d in (1, 7):
        copies["us", d, 4].wait_recv()
        gradient(d, 0)
        gradient(d, 1)
    for d in (2, 6):
        us_share(d)
    for d in (3, 5, 4):
        us_forward(d)
    gram(0)
    ct_arrived(6)
    ct_arrived(2)
    for d in (3, 5, 4):
        us_share(d)
    uf_own()
    for d in (2, 6):
        copies["us", d, 4].wait_recv()
        gradient(d, 0)
        gradient(d, 1)
    gram(1)
    gram(7)
    ct_arrived(5)
    ct_arrived(3)
    for d in (3, 5):
        copies["us", d, 4].wait_recv()
        gradient(d, 0)
        gradient(d, 1)
    gram(2)
    gram(6)
    uf_forward()
    ct_arrived(4)
    copies["us", 4, 4].wait_recv()
    gradient(4, 0)
    gradient(4, 1)
    gram(3)
    gram(5)
    gram(4)

    ones = jnp.ones((8, 128), BF16)
    sums = acc[...]
    high = sums.astype(BF16)
    low = (sums - high.astype(F32)).astype(BF16)
    over_lanes = (((1,), (1,)), ((), ()))
    flat = lax.dot_general(ones, high, over_lanes, preferred_element_type=F32) + lax.dot_general(
        ones, low, over_lanes, preferred_element_type=F32
    )
    sub = lax.broadcasted_iota(jnp.int32, (8, 128), 0)
    tile = jnp.zeros((8, 128), F32)
    for i in range(8):
        tile = jnp.where(sub == i, flat[:, i * 128 : (i + 1) * 128], tile)
    src_a[...] = tile
    stage_a = [
        send(src_a, in_a.at[k], a_s.at[k], a_r.at[k], device(dz=dz, dc=dc)) for k, (dz, dc) in enumerate(PEERS_A)
    ]

    uf_share()
    load_w.wait()
    for k in range(6, 10):
        copies["uf", k].wait_recv()
    over_width = (((1,), (1,)), ((), ()))
    parts = []
    for core in range(NC):
        rows = uf[core].reshape(NX * SHARD, D)
        parts.append(
            lax.dot_general(rows, wv[...], over_width, preferred_element_type=F32).astype(BF16)
        )
    gathered = jnp.concatenate(parts, axis=0)
    out_back[...] = lax.dot_general(pt[...], gathered, (((0,), (0,)), ((), ())), preferred_element_type=F32).astype(BF16)

    total = src_a[...]
    for k, copy in enumerate(stage_a):
        copy.wait_recv()
        total = total + in_a[k]
    src_b[...] = total
    stage_b = [
        send(src_b, in_b.at[k], b_s.at[k], b_r.at[k], device(dy=dy, dx=dx)) for k, (dy, dx) in enumerate(PEERS_B)
    ]
    for k, copy in enumerate(stage_b):
        copy.wait_recv()
        total = total + in_b[k]

    quarter = [total] + [pltpu.roll(total, 128 - N_DP * q, 1) for q in range(1, NY)]
    m = jnp.concatenate(quarter, axis=0)
    row = lax.broadcasted_iota(jnp.int32, (N_DP, 128), 0)
    lane = lax.broadcasted_iota(jnp.int32, (N_DP, 128), 1)
    m = jnp.where(lane < N_DP, m, 0.0)
    weight = jnp.ones((N_DP, 1), F32)
    for level in range(5):
        bit = 1 << level
        own = jnp.where(lane == row, m, 0.0)
        mixed = jnp.where(lane == (row ^ bit), m, 0.0)
        down = 1.0 - jnp.sum(mixed, axis=1, keepdims=True) / (2.0 * (jnp.sum(own, axis=1, keepdims=True) + EPS))
        across = 1.0 - jnp.sum(mixed, axis=0, keepdims=True) / (2.0 * (jnp.sum(own, axis=0, keepdims=True) + EPS))
        weight = weight * down
        m = (down * across) * m
        m = m + jnp.where((row & bit) == 0, pltpu.roll(m, N_DP - bit, 0), pltpu.roll(m, bit, 0))
        m = m + jnp.where((lane & bit) == 0, pltpu.roll(m, 128 - bit, 1), pltpu.roll(m, bit, 1))
        m = jnp.where(lane < N_DP, m, 0.0)
    wts[...] = jnp.broadcast_to(weight, (N_DP, 128))

    def combine(step, _):
        at = pl.ds(pl.multiple_of(step * 16, 16), 16)
        value = jnp.zeros((16, WIDE), F32)
        for b in range(N_DP):
            value = value + gv[b, at].astype(F32) * wts[b : b + 1, :]
        out_grad[at, :] = value
        return 0

    lax.fori_loop(0, HEADS // 16, combine, 0)
    for copy in started:
        copy.wait_send()


def body(context, cotangent, row_order, out_weight):
    sem = pltpu.SemaphoreType.DMA
    return pl.pallas_call(
        kernel,
        out_shape=(
            jax.ShapeDtypeStruct((HEADS, WIDE), F32),
            jax.ShapeDtypeStruct((ROWS, HEADS), BF16),
        ),
        in_specs=[pl.BlockSpec(memory_space=pl.ANY)] * 4,
        out_specs=[pl.BlockSpec(memory_space=pltpu.VMEM)] * 2,
        scratch_shapes=[
            pltpu.VMEM((NC, NX, SHARD, D), BF16),
            pltpu.VMEM((NZ, NC, NX, SHARD, SLICE), BF16),
            pltpu.VMEM((NZ - 1, SHARD, SLICE), BF16),
            pltpu.VMEM((NZ, 2, HALF, ROWS), BF16),
            pltpu.VMEM((ROWS, HEADS), BF16),
            pltpu.VMEM((1, ROWS), jnp.int32),
            pltpu.VMEM((HEADS, D), BF16),
            pltpu.VMEM((ROWS, ROWS), BF16),
            pltpu.VMEM((NZ, 2, NY, HALF, WIDE), BF16),
            pltpu.VMEM((N_DP, HEADS, WIDE), BF16),
            pltpu.VMEM((N_DP * N_DP, 128), F32),
            pltpu.VMEM((8, 128), F32),
            pltpu.VMEM((8, 128), F32),
            pltpu.VMEM((len(PEERS_A), 8, 128), F32),
            pltpu.VMEM((len(PEERS_B), 8, 128), F32),
            pltpu.VMEM((N_DP, 128), F32),
            sem((4,)),
            sem((NZ, 5)),
            sem((NZ, 5)),
            sem((NZ,)),
            sem((NZ,)),
            sem((10,)),
            sem((10,)),
            sem((NZ, 2)),
            sem((NZ, 2)),
            sem((NZ, 2, NY - 1)),
            sem((NZ, 2, NY - 1)),
            sem((len(PEERS_A),)),
            sem((len(PEERS_A),)),
            sem((len(PEERS_B),)),
            sem((len(PEERS_B),)),
        ],
        name="adasum",
        compiler_params=pltpu.CompilerParams(
            collective_id=0, has_side_effects=True, vmem_limit_bytes=48 << 20
        ),
        cost_estimate=pl.CostEstimate(flops=2_300_000_000, bytes_accessed=4_000_000, transcendentals=0),
    )(context, cotangent, row_order, out_weight)


def solution(mesh):
    in_specs = (P("dp", "tensor"), P(("dp", "tensor"), None), P("dp", None), P("tensor", None))
    out_specs = (P("tensor", "dp"), P("dp", "tensor"))
    return jax.shard_map(body, mesh=mesh, in_specs=in_specs, out_specs=out_specs, check_vma=False)
```

```python
import jax
import jax.numpy as jnp
from jax import lax
from jax.experimental import pallas as pl
from jax.experimental.pallas import tpu as pltpu
from jax.sharding import PartitionSpec as P

EPS = 1e-06
MESH = pl.DeviceIdType.MESH
BF16, F32 = jnp.bfloat16, jnp.float32
NY, NZ, NX, NC = 4, 8, 4, 2
ROWS, SHARD = 512, 64
HEADS, D = 256, 4096
SLICE = D // NZ
WIDE = D // (NY * NZ)
HALF = HEADS // 2
N_DP = NY * NZ
PEERS_A = [(dz, dc) for dz in (4, 3, 5, 2, 6, 1, 7, 0) for dc in (1, 0) if dz or dc]
PEERS_B = [(dy, dx) for dy, dx in sorted(((a, b) for a in range(NY) for b in range(NX)), key=lambda p: -min(p[0], NY - p[0]) - min(p[1], NX - p[1])) if dy or dx]
NEIGHBOURS = [(0, dz, 0, 0) for dz in (4, 3, 5, 2, 6, 1, 7)] + [(dy, 0, 0, 0) for dy in (2, 1, 3)] + [(0, 0, dx, 0) for dx in (2, 1, 3)] + [(0, 0, 0, 1)]


def kernel(
    context, cotangent, row_order, out_weight, hbm_grad, hbm_back, out_grad, out_back,
    uf, us, pack, ct, cv, ov, wv, pt, gst, gv, acc, src_a, src_b, in_a, in_b, wts,
    local, sent, us_r, aa_r, uf_r, ct_r, gv_r, ab_r,
):
    dp, tp = lax.axis_index("dp"), lax.axis_index("tensor")
    y, z = lax.div(dp, NZ), lax.rem(dp, NZ)
    x, c = lax.div(tp, NC), lax.rem(tp, NC)

    def device(dy=0, dz=0, dx=0, dc=0):
        return (
            lax.rem(y + dy, NY) * NZ + lax.rem(z + dz, NZ),
            lax.rem(x + dx, NX) * NC + lax.rem(c + dc, NC),
        )

    def send(source, target, kind, recv_sem, where):
        pltpu.make_async_remote_copy(
            src_ref=source, dst_ref=target, send_sem=sent.at[kind], recv_sem=recv_sem,
            device_id=where, device_id_type=MESH,
        ).start()

    def wait(ref, sem):
        pltpu.make_async_copy(ref, ref, sem).wait()

    barrier = pltpu.get_barrier_semaphore()
    for step in NEIGHBOURS:
        pl.semaphore_signal(barrier, inc=1, device_id=device(*step), device_id_type=MESH)

    load_cot = pltpu.make_async_copy(cotangent, uf.at[c, x], local.at[0])
    load_ctx = pltpu.make_async_copy(context, cv, local.at[1])
    load_ord = pltpu.make_async_copy(row_order, ov, local.at[2])
    load_w = pltpu.make_async_copy(out_weight, wv, local.at[3])
    load_cot.start()
    load_ctx.start()
    load_ord.start()
    load_w.start()

    load_cot.wait()
    for d in range(NZ):
        to = lax.rem(z + d, NZ)
        for j in range(NY):
            at = pl.multiple_of((j * NZ + to) * WIDE, WIDE)
            block = uf[c, x, :, pl.ds(at, WIDE)]
            if d == 0:
                us[0, c, x, :, j * WIDE : (j + 1) * WIDE] = block
            else:
                pack[d - 1, :, j * WIDE : (j + 1) * WIDE] = block

    load_ctx.wait()
    load_ord.wait()
    row = lax.broadcasted_iota(jnp.int32, (ROWS, ROWS), 0)
    name = lax.rem(lax.div(row, SHARD), NX) * (NC * SHARD) + lax.div(row, NX * SHARD) * SHARD + lax.rem(row, SHARD)
    pt[...] = (ov[...] == name).astype(F32).astype(BF16)
    mine = lax.dot_general(cv[...], pt[...], (((0,), (1,)), ((), ())), preferred_element_type=F32).astype(BF16)
    ct[0, 0] = mine[:HALF]
    ct[0, 1] = mine[HALF:]
    pl.semaphore_wait(barrier, len(NEIGHBOURS))

    right, left, sibling = device(dx=1), device(dx=NX - 1), device(dc=1)
    xl, xr, xf = lax.rem(x + NX - 1, NX), lax.rem(x + 1, NX), lax.rem(x + 2, NX)
    lo, hi = pl.ds(0, SHARD // 2), pl.ds(SHARD // 2, SHARD // 2)

    def us_own(d):
        mine = us.at[d, c, x]
        send(mine, mine, 0, us_r.at[d, 0], right)
        send(mine, mine, 0, us_r.at[d, 0], left)

    def us_forward(d):
        wait(us.at[d, c, pl.ds(0, 2)], us_r.at[d, 0])
        part = us.at[d, c, xl, lo]
        send(part, part, 0, us_r.at[d, 1], right)
        part = us.at[d, c, xr, hi]
        send(part, part, 0, us_r.at[d, 1], left)

    def us_share(d):
        wait(us.at[d, c, 0], us_r.at[d, 1])
        part = us.at[d, c]
        send(part, part, 0, us_r.at[d, 2], sibling)

    def us_ready(d):
        wait(us.at[d, c], us_r.at[d, 2])

    def aa_send(d):
        send(pack.at[d - 1], us.at[NZ - d, c, x], 1, aa_r.at[NZ - d], device(dz=d))

    def aa_ready(d):
        wait(pack.at[0], aa_r.at[d])

    def uf_own(k):
        for rows, to in ((lo, right), (hi, left)) if k == 0 else ((hi, right), (lo, left)):
            part = uf.at[c, x, rows]
            send(part, part, 2, uf_r.at[k], to)
        if k == 0:
            part = uf.at[c, x]
            send(part, part, 2, uf_r.at[3], sibling)

    def uf_forward():
        wait(uf.at[c, x], uf_r.at[0])
        part = uf.at[c, xl, lo]
        send(part, part, 2, uf_r.at[2], right)
        part = uf.at[c, xr, hi]
        send(part, part, 2, uf_r.at[2], left)

    def uf_share():
        wait(uf.at[c, x], uf_r.at[1])
        for at in (xl, xr):
            part = uf.at[c, at]
            send(part, part, 2, uf_r.at[3], sibling)
        wait(uf.at[c, x], uf_r.at[2])
        part = uf.at[c, xf]
        send(part, part, 2, uf_r.at[3], sibling)

    def ct_send(slot, h, step):
        to = (slot - step) % NZ
        send(ct.at[slot, h], ct.at[to, h], 3, ct_r.at[to, h], device(dz=step % NZ))

    def ct_arrived(d, h):
        wait(ct.at[d, h], ct_r.at[d, h])
        if d in (7, 6) or (d == 5 and h == 0):
            ct_send(d, h, 1)
        if d in (1, 2) or (d == 3 and h == 1):
            ct_send(d, h, -1)

    def replica(d, e=0):
        return lax.rem(y + e, NY) * NZ + lax.rem(z + d, NZ)

    def gv_send(d, h, e):
        target = gv.at[replica(d), pl.ds(h * HALF, HALF)]
        send(gst.at[d, h, lax.rem(y + e, NY)], target, 4, gv_r.at[d], device(dy=e))

    def gradient(d, h):
        value = jnp.dot(ct[d, h], us[d].reshape(ROWS, SLICE), preferred_element_type=F32).astype(BF16)
        for j in range(NY):
            gst[d, h, j] = value[:, j * WIDE : (j + 1) * WIDE]
        for e in (2, 1, 3):
            gv_send(d, h, e)
        gv[replica(d), h * HALF : (h + 1) * HALF] = gst[d, h, y]

    def gram_pair(d1, d2):
        first = [replica(d1, e) for e in range(NY)]
        second = [replica(d2, e) for e in range(NY)]
        pairs = [(i, j) for i in range(NY) for j in range(NY) if d1 != d2 or i <= j]

        def body(step, sums):
            at = pl.ds(pl.multiple_of(step * 16, 16), 16)
            a = [gv[b, at].astype(F32) for b in first]
            bs = a if d1 == d2 else [gv[b, at].astype(F32) for b in second]
            return tuple(s + a[i] * bs[j] for s, (i, j) in zip(sums, pairs))

        sums = lax.fori_loop(0, HEADS // 16, body, tuple(jnp.zeros((16, WIDE), F32) for _ in pairs), unroll=16)
        for s, (i, j) in zip(sums, pairs):
            line = jnp.sum(s, axis=0, keepdims=True)
            zi, yi = lax.rem(z + d1, NZ), lax.rem(y + i, NY)
            zj, yj = lax.rem(z + d2, NZ), lax.rem(y + j, NY)
            acc[pl.ds(zi * 128 + yi * N_DP + yj * NZ + zj, 1), :] = line
            acc[pl.ds(zj * 128 + yj * N_DP + yi * NZ + zi, 1), :] = line

    done = []

    def gram(d):
        wait(gv.at[pl.ds(0, NY - 1)], gv_r.at[d])
        done.append(d)
        for other in done:
            gram_pair(d, other)

    us_own(0)
    for d in (1, 7, 2, 6, 3, 5, 4):
        aa_send(d)
    us_forward(0)
    for d in (1, 7):
        aa_ready(d)
        us_own(d)
    for h in range(2):
        ct_send(0, h, 1)
        ct_send(0, h, -1)
    us_share(0)
    for d in (2, 6):
        aa_ready(d)
        us_own(d)
    us_forward(1)
    us_forward(7)
    for d in (3, 5):
        aa_ready(d)
        us_own(d)
    us_share(1)
    us_share(7)
    us_forward(2)
    us_forward(6)
    aa_ready(4)
    us_own(4)
    us_share(2)
    us_share(6)
    us_ready(0)
    gradient(0, 0)
    gradient(0, 1)
    ct_arrived(7, 0)
    ct_arrived(1, 0)
    us_forward(3)
    us_forward(5)
    ct_arrived(7, 1)
    ct_arrived(1, 1)
    us_forward(4)
    us_share(3)
    us_share(5)
    for d in (1, 7):
        us_ready(d)
        gradient(d, 0)
        gradient(d, 1)
    us_share(4)
    uf_own(0)
    uf_own(1)
    us_ready(2)
    us_ready(6)
    for h in range(2):
        ct_arrived(6, h)
        ct_arrived(2, h)
        gradient(6, h)
        gradient(2, h)
    gram(0)
    gram(1)
    uf_forward()
    us_ready(3)
    us_ready(5)
    for h in range(2):
        ct_arrived(5, h)
        ct_arrived(3, h)
        gradient(5, h)
        gradient(3, h)
        if h == 0:
            gram(7)
    gram(2)
    gram(6)
    us_ready(4)
    for h in range(2):
        ct_arrived(4, h)
        gradient(4, h)
    uf_share()
    gram(3)
    gram(5)
    gram(4)

    ones = jnp.ones((8, 128), BF16)
    sums = acc[...]
    high = sums.astype(BF16)
    low = (sums - high.astype(F32)).astype(BF16)
    over_lanes = (((1,), (1,)), ((), ()))
    flat = lax.dot_general(ones, high, over_lanes, preferred_element_type=F32) + lax.dot_general(
        ones, low, over_lanes, preferred_element_type=F32
    )
    sub = lax.broadcasted_iota(jnp.int32, (8, 128), 0)
    tile = jnp.zeros((8, 128), F32)
    for i in range(8):
        tile = jnp.where(sub == i, flat[:, i * 128 : (i + 1) * 128], tile)
    src_a[...] = tile
    for k, (dz, dc) in enumerate(PEERS_A):
        send(src_a, in_a.at[k], 5, ab_r.at[0], device(dz=dz, dc=dc))

    load_w.wait()
    wait(uf.at[c], uf_r.at[3])
    over_width = (((1,), (1,)), ((), ()))
    parts = []
    for core in range(NC):
        rows = uf[core].reshape(NX * SHARD, D)
        parts.append(
            lax.dot_general(rows, wv[...], over_width, preferred_element_type=F32).astype(BF16)
        )
    gathered = jnp.concatenate(parts, axis=0)
    out_back[...] = lax.dot_general(pt[...], gathered, (((0,), (0,)), ((), ())), preferred_element_type=F32).astype(BF16)

    store_back = pltpu.make_async_copy(out_back, hbm_back, local.at[4])
    store_back.start()

    wait(in_a, ab_r.at[0])
    total = src_a[...]
    for k in range(len(PEERS_A)):
        total = total + in_a[k]
    src_b[...] = total
    for k, (dy, dx) in enumerate(PEERS_B):
        send(src_b, in_b.at[k], 6, ab_r.at[1], device(dy=dy, dx=dx))
    wait(in_b, ab_r.at[1])
    for k in range(len(PEERS_B)):
        total = total + in_b[k]

    quarter = [total] + [pltpu.roll(total, 128 - N_DP * q, 1) for q in range(1, NY)]
    m = jnp.concatenate(quarter, axis=0)
    row = lax.broadcasted_iota(jnp.int32, (N_DP, 128), 0)
    lane = lax.broadcasted_iota(jnp.int32, (N_DP, 128), 1)
    m = jnp.where(lane < N_DP, m, 0.0)
    weight = jnp.ones((N_DP, 1), F32)
    for level in range(5):
        bit = 1 << level
        own = jnp.where(lane == row, m, 0.0)
        mixed = jnp.where(lane == (row ^ bit), m, 0.0)
        down = 1.0 - jnp.sum(mixed, axis=1, keepdims=True) / (2.0 * (jnp.sum(own, axis=1, keepdims=True) + EPS))
        across = 1.0 - jnp.sum(mixed, axis=0, keepdims=True) / (2.0 * (jnp.sum(own, axis=0, keepdims=True) + EPS))
        weight = weight * down
        m = (down * across) * m
        m = m + jnp.where((row & bit) == 0, pltpu.roll(m, N_DP - bit, 0), pltpu.roll(m, bit, 0))
        m = m + jnp.where((lane & bit) == 0, pltpu.roll(m, 128 - bit, 1), pltpu.roll(m, bit, 1))
        m = jnp.where(lane < N_DP, m, 0.0)
    wts[...] = jnp.broadcast_to(weight, (N_DP, 128))

    def combine(step, _):
        at = pl.ds(pl.multiple_of(step * 16, 16), 16)
        value = jnp.zeros((16, WIDE), F32)
        for b in range(N_DP):
            value = value + gv[b, at].astype(F32) * wts[b : b + 1, :]
        out_grad[at, :] = value
        return 0

    lax.fori_loop(0, HEADS // 16, combine, 0, unroll=4)
    store_grad = pltpu.make_async_copy(out_grad, hbm_grad, local.at[5])
    store_grad.start()
    whole = (us.at[pl.ds(0, 7)], pack, us.at[pl.ds(0, 7)], ct.at[pl.ds(0, 7)], gv.at[pl.ds(0, 24)], in_a, in_b)
    for kind, ref in enumerate(whole):
        wait(ref, sent.at[kind])
    store_grad.wait()
    store_back.wait()


def hand_over(grad, back, out_grad, out_back):
    out_grad[...] = grad[...]
    out_back[...] = back[...]


def body(context, cotangent, row_order, out_weight):
    sem = pltpu.SemaphoreType.DMA
    grad, back = pl.pallas_call(
        kernel,
        out_shape=(
            jax.ShapeDtypeStruct((HEADS, WIDE), F32),
            jax.ShapeDtypeStruct((ROWS, HEADS), BF16),
        ),
        in_specs=[pl.BlockSpec(memory_space=pl.ANY)] * 4,
        out_specs=[pl.BlockSpec(memory_space=pltpu.HBM)] * 2,
        scratch_shapes=[
            pltpu.VMEM((HEADS, WIDE), F32),
            pltpu.VMEM((ROWS, HEADS), BF16),
            pltpu.VMEM((NC, NX, SHARD, D), BF16),
            pltpu.VMEM((NZ, NC, NX, SHARD, SLICE), BF16),
            pltpu.VMEM((NZ - 1, SHARD, SLICE), BF16),
            pltpu.VMEM((NZ, 2, HALF, ROWS), BF16),
            pltpu.VMEM((ROWS, HEADS), BF16),
            pltpu.VMEM((1, ROWS), jnp.int32),
            pltpu.VMEM((HEADS, D), BF16),
            pltpu.VMEM((ROWS, ROWS), BF16),
            pltpu.VMEM((NZ, 2, NY, HALF, WIDE), BF16),
            pltpu.VMEM((N_DP, HEADS, WIDE), BF16),
            pltpu.VMEM((N_DP * N_DP, 128), F32),
            pltpu.VMEM((8, 128), F32),
            pltpu.VMEM((8, 128), F32),
            pltpu.VMEM((len(PEERS_A), 8, 128), F32),
            pltpu.VMEM((len(PEERS_B), 8, 128), F32),
            pltpu.VMEM((N_DP, 128), F32),
            sem((6,)),
            sem((7,)),
            sem((NZ, 3)),
            sem((NZ,)),
            sem((4,)),
            sem((NZ, 2)),
            sem((NZ,)),
            sem((2,)),
        ],
        name="adasum",
        compiler_params=pltpu.CompilerParams(
            collective_id=0, has_side_effects=True, vmem_limit_bytes=63 << 20
        ),
        cost_estimate=pl.CostEstimate(flops=2_300_000_000, bytes_accessed=4_000_000, transcendentals=0),
    )(context, cotangent, row_order, out_weight)
    return pl.pallas_call(
        hand_over,
        out_shape=(jax.ShapeDtypeStruct(grad.shape, F32), jax.ShapeDtypeStruct(back.shape, BF16)),
        name="hand_over",
    )(grad, back)


def solution(mesh):
    in_specs = (P("dp", "tensor"), P(("dp", "tensor"), None), P("dp", None), P("tensor", None))
    out_specs = (P("tensor", "dp"), P("dp", "tensor"))
    return jax.shard_map(body, mesh=mesh, in_specs=in_specs, out_specs=out_specs, check_vma=False)
```

```python
import jax
import jax.numpy as jnp
from jax import lax
from jax.experimental import pallas as pl
from jax.experimental.pallas import tpu as pltpu
from jax.sharding import PartitionSpec as P

EPS = 1e-06
MESH = pl.DeviceIdType.MESH
BF16, F32 = jnp.bfloat16, jnp.float32
NY, NZ, NX, NC = 4, 8, 4, 2
ROWS, SHARD = 512, 64
HEADS, D = 256, 4096
SLICE = D // NZ
WIDE = D // (NY * NZ)
HALF = HEADS // 2
N_DP = NY * NZ
PEERS_A = [(dz, dc) for dz in (4, 3, 5, 2, 6, 1, 7, 0) for dc in (1, 0) if dz or dc]
PEERS_B = [(dy, dx) for dy, dx in sorted(((a, b) for a in range(NY) for b in range(NX)), key=lambda p: -min(p[0], NY - p[0]) - min(p[1], NX - p[1])) if dy or dx]
NEIGHBOURS = [(0, dz, 0, 0) for dz in (4, 3, 5, 2, 6, 1, 7)] + [(dy, 0, 0, 0) for dy in (2, 1, 3)] + [(0, 0, dx, 0) for dx in (2, 1, 3)] + [(0, 0, 0, 1)]


def kernel(
    context, cotangent, row_order, out_weight, out_grad, out_back,
    uf, us, pack, ct, cv, ov, wv, pt, gst, gv, acc, src_a, src_b, in_a, in_b, wts,
    local, sent, us_r, aa_r, uf_r, ct_r, gv_r, ab_r,
):
    dp, tp = lax.axis_index("dp"), lax.axis_index("tensor")
    y, z = lax.div(dp, NZ), lax.rem(dp, NZ)
    x, c = lax.div(tp, NC), lax.rem(tp, NC)

    def device(dy=0, dz=0, dx=0, dc=0):
        return (
            lax.rem(y + dy, NY) * NZ + lax.rem(z + dz, NZ),
            lax.rem(x + dx, NX) * NC + lax.rem(c + dc, NC),
        )

    def send(source, target, kind, recv_sem, where):
        pltpu.make_async_remote_copy(
            src_ref=source, dst_ref=target, send_sem=sent.at[kind], recv_sem=recv_sem,
            device_id=where, device_id_type=MESH,
        ).start()

    def wait(ref, sem):
        pltpu.make_async_copy(ref, ref, sem).wait()

    barrier = pltpu.get_barrier_semaphore()
    for step in NEIGHBOURS:
        pl.semaphore_signal(barrier, inc=1, device_id=device(*step), device_id_type=MESH)

    load_cot = pltpu.make_async_copy(cotangent, uf.at[c, x], local.at[0])
    load_ctx = pltpu.make_async_copy(context, cv, local.at[1])
    load_ord = pltpu.make_async_copy(row_order, ov, local.at[2])
    load_w = pltpu.make_async_copy(out_weight, wv, local.at[3])
    load_cot.start()
    load_ctx.start()
    load_ord.start()
    load_w.start()

    load_cot.wait()
    for d in range(NZ):
        to = lax.rem(z + d, NZ)
        for j in range(NY):
            at = pl.multiple_of((j * NZ + to) * WIDE, WIDE)
            block = uf[c, x, :, pl.ds(at, WIDE)]
            if d == 0:
                us[0, c, x, :, j * WIDE : (j + 1) * WIDE] = block
            else:
                pack[d - 1, :, j * WIDE : (j + 1) * WIDE] = block

    load_ctx.wait()
    load_ord.wait()
    row = lax.broadcasted_iota(jnp.int32, (ROWS, ROWS), 0)
    name = lax.rem(lax.div(row, SHARD), NX) * (NC * SHARD) + lax.div(row, NX * SHARD) * SHARD + lax.rem(row, SHARD)
    pt[...] = (ov[...] == name).astype(F32).astype(BF16)
    mine = lax.dot_general(cv[...], pt[...], (((0,), (1,)), ((), ())), preferred_element_type=F32).astype(BF16)
    ct[0, 0] = mine[:HALF]
    ct[0, 1] = mine[HALF:]
    pl.semaphore_wait(barrier, len(NEIGHBOURS))

    right, left, far, sibling = device(dx=1), device(dx=NX - 1), device(dx=2), device(dc=1)
    xl, xr, xf = lax.rem(x + NX - 1, NX), lax.rem(x + 1, NX), lax.rem(x + 2, NX)
    lo, hi = pl.ds(0, SHARD // 2), pl.ds(SHARD // 2, SHARD // 2)

    def us_own(d):
        mine = us.at[d, c, x]
        for to in (far, right, left):
            send(mine, mine, 0, us_r.at[d, 0], to)

    def us_share(d):
        wait(us.at[d, c, pl.ds(0, 3)], us_r.at[d, 0])
        part = us.at[d, c]
        send(part, part, 0, us_r.at[d, 1], sibling)

    def us_ready(d):
        wait(us.at[d, c], us_r.at[d, 1])

    def aa_send(d):
        send(pack.at[d - 1], us.at[NZ - d, c, x], 1, aa_r.at[NZ - d], device(dz=d))

    def aa_ready(d):
        wait(pack.at[0], aa_r.at[d])

    def uf_own(k):
        for rows, to in ((lo, right), (hi, left)) if k == 0 else ((hi, right), (lo, left)):
            part = uf.at[c, x, rows]
            send(part, part, 2, uf_r.at[k], to)
        if k == 0:
            part = uf.at[c, x]
            send(part, part, 2, uf_r.at[3], sibling)

    def uf_forward():
        wait(uf.at[c, x], uf_r.at[0])
        part = uf.at[c, xl, lo]
        send(part, part, 2, uf_r.at[2], right)
        part = uf.at[c, xr, hi]
        send(part, part, 2, uf_r.at[2], left)

    def uf_share_near():
        wait(uf.at[c, x], uf_r.at[1])
        for at in (xl, xr):
            part = uf.at[c, at]
            send(part, part, 2, uf_r.at[3], sibling)

    def uf_share_far():
        wait(uf.at[c, x], uf_r.at[2])
        part = uf.at[c, xf]
        send(part, part, 2, uf_r.at[3], sibling)

    def ct_send(slot, h, step):
        to = (slot - step) % NZ
        send(ct.at[slot, h], ct.at[to, h], 3, ct_r.at[to, h], device(dz=step % NZ))

    def ct_arrived(d, h):
        wait(ct.at[d, h], ct_r.at[d, h])
        if d in (7, 6) or (d == 5 and h == 0):
            ct_send(d, h, 1)
        if d in (1, 2) or (d == 3 and h == 1):
            ct_send(d, h, -1)

    def replica(d, e=0):
        return lax.rem(y + e, NY) * NZ + lax.rem(z + d, NZ)

    def gv_send(d, h, e):
        target = gv.at[replica(d), pl.ds(h * HALF, HALF)]
        send(gst.at[d, h, lax.rem(y + e, NY)], target, 4, gv_r.at[d], device(dy=e))

    def gradient(d, h):
        value = jnp.dot(ct[d, h], us[d].reshape(ROWS, SLICE), preferred_element_type=F32).astype(BF16)
        for j in range(NY):
            gst[d, h, j] = value[:, j * WIDE : (j + 1) * WIDE]
        for e in (2, 1, 3):
            gv_send(d, h, e)
        gv[replica(d), h * HALF : (h + 1) * HALF] = gst[d, h, y]

    def gram_pair(d1, d2):
        first = [replica(d1, e) for e in range(NY)]
        second = [replica(d2, e) for e in range(NY)]
        pairs = [(i, j) for i in range(NY) for j in range(NY) if d1 != d2 or i <= j]

        def body(step, sums):
            at = pl.ds(pl.multiple_of(step * 16, 16), 16)
            a = [gv[b, at].astype(F32) for b in first]
            bs = a if d1 == d2 else [gv[b, at].astype(F32) for b in second]
            return tuple(s + a[i] * bs[j] for s, (i, j) in zip(sums, pairs))

        sums = lax.fori_loop(0, HEADS // 16, body, tuple(jnp.zeros((16, WIDE), F32) for _ in pairs), unroll=16)
        for s, (i, j) in zip(sums, pairs):
            line = jnp.sum(s, axis=0, keepdims=True)
            zi, yi = lax.rem(z + d1, NZ), lax.rem(y + i, NY)
            zj, yj = lax.rem(z + d2, NZ), lax.rem(y + j, NY)
            acc[pl.ds(zi * 128 + yi * N_DP + yj * NZ + zj, 1), :] = line
            acc[pl.ds(zj * 128 + yj * N_DP + yi * NZ + zi, 1), :] = line

    done = []

    def gram(d):
        wait(gv.at[pl.ds(0, NY - 1)], gv_r.at[d])
        done.append(d)
        for other in done:
            gram_pair(d, other)

    us_own(0)
    for d in (1, 7, 2, 6):
        aa_send(d)
    for h in range(2):
        ct_send(0, h, 1)
        ct_send(0, 1 - h, -1)
    for d in (1, 7):
        aa_ready(d)
        us_own(d)
    us_share(0)
    for d in (2, 6):
        aa_ready(d)
        us_own(d)
    for d in (3, 5, 4):
        aa_send(d)
    us_share(1)
    us_share(7)
    us_ready(0)
    gradient(0, 0)
    gradient(0, 1)
    us_share(2)
    us_share(6)
    for h in range(2):
        ct_arrived(7, h)
        ct_arrived(1, 1 - h)
    us_ready(1)
    us_ready(7)
    for h in range(2):
        gradient(7, h)
        gradient(1, 1 - h)
    for d in (3, 5):
        aa_ready(d)
        us_own(d)
    aa_ready(4)
    us_own(4)
    us_ready(2)
    us_ready(6)
    ct_arrived(6, 0)
    ct_arrived(2, 1)
    gradient(6, 0)
    gradient(2, 1)
    ct_arrived(6, 1)
    ct_arrived(2, 0)
    gradient(6, 1)
    gradient(2, 0)
    us_share(3)
    us_share(5)
    gram(0)
    gram(1)
    us_share(4)
    uf_own(0)
    uf_own(1)
    us_ready(3)
    us_ready(5)
    ct_arrived(5, 0)
    ct_arrived(3, 1)
    gradient(5, 0)
    gradient(3, 1)
    gram(7)
    ct_arrived(5, 1)
    ct_arrived(3, 0)
    gradient(5, 1)
    gradient(3, 0)
    us_ready(4)
    gram(2)
    gram(6)
    ct_arrived(4, 0)
    gradient(4, 0)
    ct_arrived(4, 1)
    gradient(4, 1)
    uf_forward()
    gram(3)
    gram(5)
    gram(4)

    ones = jnp.ones((8, 128), BF16)
    sums = acc[...]
    high = sums.astype(BF16)
    low = (sums - high.astype(F32)).astype(BF16)
    over_lanes = (((1,), (1,)), ((), ()))
    flat = lax.dot_general(ones, high, over_lanes, preferred_element_type=F32) + lax.dot_general(
        ones, low, over_lanes, preferred_element_type=F32
    )
    sub = lax.broadcasted_iota(jnp.int32, (8, 128), 0)
    tile = jnp.zeros((8, 128), F32)
    for i in range(8):
        tile = jnp.where(sub == i, flat[:, i * 128 : (i + 1) * 128], tile)
    src_a[...] = tile
    for k, (dz, dc) in enumerate(PEERS_A):
        send(src_a, in_a.at[k], 5, ab_r.at[0], device(dz=dz, dc=dc))

    uf_share_near()
    wait(in_a, ab_r.at[0])
    total = src_a[...]
    for k in range(len(PEERS_A)):
        total = total + in_a[k]
    src_b[...] = total
    for k, (dy, dx) in enumerate(PEERS_B):
        send(src_b, in_b.at[k], 6, ab_r.at[1], device(dy=dy, dx=dx))
    uf_share_far()
    load_w.wait()
    wait(uf.at[c], uf_r.at[3])
    over_width = (((1,), (1,)), ((), ()))
    parts = []
    for core in range(NC):
        rows = uf[core].reshape(NX * SHARD, D)
        parts.append(
            lax.dot_general(rows, wv[...], over_width, preferred_element_type=F32).astype(BF16)
        )
    gathered = jnp.concatenate(parts, axis=0)
    out_back[...] = lax.dot_general(pt[...], gathered, (((0,), (0,)), ((), ())), preferred_element_type=F32).astype(BF16)

    wait(in_b, ab_r.at[1])
    for k in range(len(PEERS_B)):
        total = total + in_b[k]

    quarter = [total] + [pltpu.roll(total, 128 - N_DP * q, 1) for q in range(1, NY)]
    m = jnp.concatenate(quarter, axis=0)
    row = lax.broadcasted_iota(jnp.int32, (N_DP, 128), 0)
    lane = lax.broadcasted_iota(jnp.int32, (N_DP, 128), 1)
    m = jnp.where(lane < N_DP, m, 0.0)
    weight = jnp.ones((N_DP, 1), F32)
    for level in range(5):
        bit = 1 << level
        own = jnp.where(lane == row, m, 0.0)
        mixed = jnp.where(lane == (row ^ bit), m, 0.0)
        down = 1.0 - jnp.sum(mixed, axis=1, keepdims=True) / (2.0 * (jnp.sum(own, axis=1, keepdims=True) + EPS))
        across = 1.0 - jnp.sum(mixed, axis=0, keepdims=True) / (2.0 * (jnp.sum(own, axis=0, keepdims=True) + EPS))
        weight = weight * down
        m = (down * across) * m
        m = m + jnp.where((row & bit) == 0, pltpu.roll(m, N_DP - bit, 0), pltpu.roll(m, bit, 0))
        m = m + jnp.where((lane & bit) == 0, pltpu.roll(m, 128 - bit, 1), pltpu.roll(m, bit, 1))
        m = jnp.where(lane < N_DP, m, 0.0)
    wts[...] = jnp.broadcast_to(weight, (N_DP, 128))

    def combine(step, _):
        at = pl.ds(pl.multiple_of(step * 16, 16), 16)
        value = jnp.zeros((16, WIDE), F32)
        for b in range(N_DP):
            value = value + gv[b, at].astype(F32) * wts[b : b + 1, :]
        out_grad[at, :] = value
        return 0

    lax.fori_loop(0, HEADS // 16, combine, 0, unroll=4)
    whole = (us.at[pl.ds(0, 7)], pack, us.at[pl.ds(0, 7)], ct.at[pl.ds(0, 7)], gv.at[pl.ds(0, 24)], in_a, in_b)
    for kind, ref in enumerate(whole):
        wait(ref, sent.at[kind])


def body(context, cotangent, row_order, out_weight):
    sem = pltpu.SemaphoreType.DMA
    grad, back = pl.pallas_call(
        kernel,
        out_shape=(
            jax.ShapeDtypeStruct((HEADS, WIDE), F32),
            jax.ShapeDtypeStruct((ROWS, HEADS), BF16),
        ),
        in_specs=[pl.BlockSpec(memory_space=pl.ANY)] * 4,
        out_specs=[pl.BlockSpec(memory_space=pltpu.VMEM)] * 2,
        scratch_shapes=[
            pltpu.VMEM((NC, NX, SHARD, D), BF16),
            pltpu.VMEM((NZ, NC, NX, SHARD, SLICE), BF16),
            pltpu.VMEM((NZ - 1, SHARD, SLICE), BF16),
            pltpu.VMEM((NZ, 2, HALF, ROWS), BF16),
            pltpu.VMEM((ROWS, HEADS), BF16),
            pltpu.VMEM((1, ROWS), jnp.int32),
            pltpu.VMEM((HEADS, D), BF16),
            pltpu.VMEM((ROWS, ROWS), BF16),
            pltpu.VMEM((NZ, 2, NY, HALF, WIDE), BF16),
            pltpu.VMEM((N_DP, HEADS, WIDE), BF16),
            pltpu.VMEM((N_DP * N_DP, 128), F32),
            pltpu.VMEM((8, 128), F32),
            pltpu.VMEM((8, 128), F32),
            pltpu.VMEM((len(PEERS_A), 8, 128), F32),
            pltpu.VMEM((len(PEERS_B), 8, 128), F32),
            pltpu.VMEM((N_DP, 128), F32),
            sem((4,)),
            sem((7,)),
            sem((NZ, 2)),
            sem((NZ,)),
            sem((4,)),
            sem((NZ, 2)),
            sem((NZ,)),
            sem((2,)),
        ],
        name="adasum",
        compiler_params=pltpu.CompilerParams(
            collective_id=0, has_side_effects=True, vmem_limit_bytes=int(53.5 * 2**20)
        ),
        cost_estimate=pl.CostEstimate(flops=2_300_000_000, bytes_accessed=4_000_000, transcendentals=0),
    )(context, cotangent, row_order, out_weight)
    return grad, back


def solution(mesh):
    in_specs = (P("dp", "tensor"), P(("dp", "tensor"), None), P("dp", None), P("tensor", None))
    out_specs = (P("tensor", "dp"), P("dp", "tensor"))
    return jax.shard_map(body, mesh=mesh, in_specs=in_specs, out_specs=out_specs, check_vma=False)
```

```python
import jax
import jax.numpy as jnp
from jax import lax
from jax.experimental import pallas as pl
from jax.experimental.pallas import tpu as pltpu
from jax.sharding import PartitionSpec as P

EPS = 1e-06
MESH = pl.DeviceIdType.MESH
BF16, F32 = jnp.bfloat16, jnp.float32
NY, NZ, NX, NC = 4, 8, 4, 2
ROWS, SHARD = 512, 64
HEADS, D = 256, 4096
SLICE = D // NZ
WIDE = D // (NY * NZ)
HALF = HEADS // 2
N_DP = NY * NZ
PEERS_A = [(dz, dc) for dz in (4, 3, 5, 2, 6, 1, 7, 0) for dc in (1, 0) if dz or dc]
PEERS_B = [(dy, dx) for dy, dx in sorted(((a, b) for a in range(NY) for b in range(NX)), key=lambda p: -min(p[0], NY - p[0]) - min(p[1], NX - p[1])) if dy or dx]
NEIGHBOURS = [(0, dz, 0, 0) for dz in (2, 6, 1, 7)] + [(dy, 0, 0, 0) for dy in (2, 1, 3)] + [(0, 0, dx, 0) for dx in (2, 1, 3)] + [(0, 0, 0, 1)]


def kernel(
    context, cotangent, row_order, out_weight, out_grad, out_back,
    uf, us, pack, ct, cv, ov, wv, pt, gst, gv, acc, src_a, src_b, in_a, in_b, wts,
    local, sent, us_r, aa_r, uf_r, ct_r, gv_r, ab_r,
):
    dp, tp = lax.axis_index("dp"), lax.axis_index("tensor")
    y, z = lax.div(dp, NZ), lax.rem(dp, NZ)
    x, c = lax.div(tp, NC), lax.rem(tp, NC)

    def device(dy=0, dz=0, dx=0, dc=0):
        return (
            lax.rem(y + dy, NY) * NZ + lax.rem(z + dz, NZ),
            lax.rem(x + dx, NX) * NC + lax.rem(c + dc, NC),
        )

    def send(source, target, kind, recv_sem, where):
        pltpu.make_async_remote_copy(
            src_ref=source, dst_ref=target, send_sem=sent.at[kind], recv_sem=recv_sem,
            device_id=where, device_id_type=MESH,
        ).start()

    def wait(ref, sem):
        pltpu.make_async_copy(ref, ref, sem).wait()

    barrier = pltpu.get_barrier_semaphore()
    for step in NEIGHBOURS:
        pl.semaphore_signal(barrier, inc=1, device_id=device(*step), device_id_type=MESH)

    load_cot = pltpu.make_async_copy(cotangent, uf.at[c, x], local.at[0])
    load_ctx = pltpu.make_async_copy(context, cv, local.at[1])
    load_ord = pltpu.make_async_copy(row_order, ov, local.at[2])
    load_w = pltpu.make_async_copy(out_weight, wv, local.at[3])
    load_cot.start()
    load_ctx.start()
    load_ord.start()
    load_w.start()

    load_cot.wait()
    for d in range(NZ):
        to = lax.rem(z + d, NZ)
        for j in range(NY):
            at = pl.multiple_of((j * NZ + to) * WIDE, WIDE)
            block = uf[c, x, :, pl.ds(at, WIDE)]
            if d == 0:
                us[0, c, x, :, j * WIDE : (j + 1) * WIDE] = block
            else:
                pack[d - 1, :, j * WIDE : (j + 1) * WIDE] = block

    load_ctx.wait()
    load_ord.wait()
    row = lax.broadcasted_iota(jnp.int32, (ROWS, ROWS), 0)
    name = lax.rem(lax.div(row, SHARD), NX) * (NC * SHARD) + lax.div(row, NX * SHARD) * SHARD + lax.rem(row, SHARD)
    pt[...] = (ov[...] == name).astype(F32).astype(BF16)
    mine = lax.dot_general(cv[...], pt[...], (((0,), (1,)), ((), ())), preferred_element_type=F32).astype(BF16)
    ct[0, 0] = mine[:HALF]
    ct[0, 1] = mine[HALF:]
    pl.semaphore_wait(barrier, len(NEIGHBOURS))

    right, left, far, sibling = device(dx=1), device(dx=NX - 1), device(dx=2), device(dc=1)
    xl, xr, xf = lax.rem(x + NX - 1, NX), lax.rem(x + 1, NX), lax.rem(x + 2, NX)
    lo, hi = pl.ds(0, SHARD // 2), pl.ds(SHARD // 2, SHARD // 2)

    def us_own(d):
        mine = us.at[d, c, x]
        for to in (far, right, left):
            send(mine, mine, 0, us_r.at[d, 0], to)

    def us_share(d):
        wait(us.at[d, c, pl.ds(0, 3)], us_r.at[d, 0])
        part = us.at[d, c]
        send(part, part, 0, us_r.at[d, 1], sibling)

    def us_ready(d):
        wait(us.at[d, c], us_r.at[d, 1])

    def aa_send(d):
        send(pack.at[d - 1], us.at[NZ - d, c, x], 1, aa_r.at[NZ - d], device(dz=d))

    def aa_ready(d):
        wait(pack.at[0], aa_r.at[d])

    def uf_own(k):
        for rows, to in ((lo, right), (hi, left)) if k == 0 else ((hi, right), (lo, left)):
            part = uf.at[c, x, rows]
            send(part, part, 2, uf_r.at[k], to)
        if k == 0:
            part = uf.at[c, x]
            send(part, part, 2, uf_r.at[3], sibling)

    def uf_forward():
        wait(uf.at[c, x], uf_r.at[0])
        part = uf.at[c, xl, lo]
        send(part, part, 2, uf_r.at[2], right)
        part = uf.at[c, xr, hi]
        send(part, part, 2, uf_r.at[2], left)

    def uf_share_near():
        wait(uf.at[c, x], uf_r.at[1])
        for at in (xl, xr):
            part = uf.at[c, at]
            send(part, part, 2, uf_r.at[3], sibling)

    def uf_share_far():
        wait(uf.at[c, x], uf_r.at[2])
        part = uf.at[c, xf]
        send(part, part, 2, uf_r.at[3], sibling)

    def ct_send(slot, h, step):
        to = (slot - step) % NZ
        send(ct.at[slot, h], ct.at[to, h], 3, ct_r.at[to, h], device(dz=step % NZ))

    def ct_arrived(d, h):
        wait(ct.at[d, h], ct_r.at[d, h])
        if d in (7, 6) or (d == 5 and h == 0):
            ct_send(d, h, 1)
        if d in (1, 2) or (d == 3 and h == 1):
            ct_send(d, h, -1)

    def replica(d, e=0):
        return lax.rem(y + e, NY) * NZ + lax.rem(z + d, NZ)

    def gv_send(d, h, e):
        target = gv.at[replica(d), pl.ds(h * HALF, HALF)]
        send(gst.at[d, h, lax.rem(y + e, NY)], target, 4, gv_r.at[d, h], device(dy=e))

    def gradient(d, h):
        value = jnp.dot(ct[d, h], us[d].reshape(ROWS, SLICE), preferred_element_type=F32).astype(BF16)
        for j in range(NY):
            gst[d, h, j] = value[:, j * WIDE : (j + 1) * WIDE]
        for e in (2, 1, 3):
            gv_send(d, h, e)
        gv[replica(d), h * HALF : (h + 1) * HALF] = gst[d, h, y]

    def gram_pair(d1, d2, h):
        first = [replica(d1, e) for e in range(NY)]
        second = [replica(d2, e) for e in range(NY)]
        pairs = [(i, j) for i in range(NY) for j in range(NY) if d1 != d2 or i <= j]

        def body(step, sums):
            at = pl.ds(pl.multiple_of(h * HALF + step * 16, 16), 16)
            a = [gv[b, at].astype(F32) for b in first]
            bs = a if d1 == d2 else [gv[b, at].astype(F32) for b in second]
            return tuple(s + a[i] * bs[j] for s, (i, j) in zip(sums, pairs))

        sums = lax.fori_loop(0, HALF // 16, body, tuple(jnp.zeros((16, WIDE), F32) for _ in pairs), unroll=8)
        for s, (i, j) in zip(sums, pairs):
            line = jnp.sum(s, axis=0, keepdims=True)
            zi, yi = lax.rem(z + d1, NZ), lax.rem(y + i, NY)
            zj, yj = lax.rem(z + d2, NZ), lax.rem(y + j, NY)
            acc[h, pl.ds(zi * 128 + yi * N_DP + yj * NZ + zj, 1), :] = line
            acc[h, pl.ds(zj * 128 + yj * N_DP + yi * NZ + zi, 1), :] = line

    done = ([], [])

    def gram_half(d, h):
        wait(gv.at[pl.ds(0, NY - 1), pl.ds(0, HALF)], gv_r.at[d, h])
        done[h].append(d)
        for other in done[h]:
            gram_pair(d, other, h)

    def gram(d):
        for h in range(2):
            gram_half(d, h)

    us_own(0)
    for d in (1, 7, 2, 6):
        aa_send(d)
    for h in range(2):
        ct_send(0, h, 1)
        ct_send(0, 1 - h, -1)
    for d in (1, 7):
        aa_ready(d)
        us_own(d)
    us_share(0)
    for d in (2, 6):
        aa_ready(d)
        us_own(d)
    for d in (3, 5, 4):
        aa_send(d)
    us_share(1)
    us_share(7)
    us_ready(0)
    gradient(0, 0)
    gradient(0, 1)
    us_share(2)
    us_share(6)
    for h in range(2):
        ct_arrived(7, h)
        ct_arrived(1, 1 - h)
    us_ready(1)
    us_ready(7)
    for h in range(2):
        gradient(7, h)
        gradient(1, 1 - h)
    for d in (3, 5):
        aa_ready(d)
        us_own(d)
    aa_ready(4)
    us_own(4)
    us_ready(2)
    us_ready(6)
    ct_arrived(6, 0)
    ct_arrived(2, 1)
    gradient(6, 0)
    gradient(2, 1)
    us_share(3)
    us_share(5)
    ct_arrived(6, 1)
    ct_arrived(2, 0)
    gradient(6, 1)
    gradient(2, 0)
    gram(0)
    gram(1)
    us_share(4)
    uf_own(0)
    uf_own(1)
    us_ready(3)
    us_ready(5)
    ct_arrived(5, 0)
    ct_arrived(3, 1)
    gradient(5, 0)
    gradient(3, 1)
    gram(7)
    ct_arrived(5, 1)
    ct_arrived(3, 0)
    gradient(5, 1)
    gradient(3, 0)
    us_ready(4)
    gram(2)
    gram(6)
    ct_arrived(4, 0)
    gradient(4, 0)
    ct_arrived(4, 1)
    gradient(4, 1)
    uf_forward()
    gram_half(5, 0)
    gram_half(3, 1)
    gram_half(5, 1)
    gram_half(3, 0)
    gram_half(4, 0)
    gram_half(4, 1)

    ones = jnp.ones((8, 128), BF16)
    sums = acc[0] + acc[1]
    high = sums.astype(BF16)
    low = (sums - high.astype(F32)).astype(BF16)
    over_lanes = (((1,), (1,)), ((), ()))
    flat = lax.dot_general(ones, high, over_lanes, preferred_element_type=F32) + lax.dot_general(
        ones, low, over_lanes, preferred_element_type=F32
    )
    sub = lax.broadcasted_iota(jnp.int32, (8, 128), 0)
    tile = jnp.zeros((8, 128), F32)
    for i in range(8):
        tile = jnp.where(sub == i, flat[:, i * 128 : (i + 1) * 128], tile)
    src_a[...] = tile
    for k, (dz, dc) in enumerate(PEERS_A):
        send(src_a, in_a.at[k], 5, ab_r.at[0], device(dz=dz, dc=dc))

    uf_share_near()
    wait(in_a, ab_r.at[0])
    total = src_a[...]
    for k in range(len(PEERS_A)):
        total = total + in_a[k]
    src_b[...] = total
    for k, (dy, dx) in enumerate(PEERS_B):
        send(src_b, in_b.at[k], 6, ab_r.at[1], device(dy=dy, dx=dx))
    uf_share_far()
    load_w.wait()
    wait(uf.at[c], uf_r.at[3])
    over_width = (((1,), (1,)), ((), ()))
    parts = []
    for core in range(NC):
        rows = uf[core].reshape(NX * SHARD, D)
        parts.append(
            lax.dot_general(rows, wv[...], over_width, preferred_element_type=F32).astype(BF16)
        )
    gathered = jnp.concatenate(parts, axis=0)
    out_back[...] = lax.dot_general(pt[...], gathered, (((0,), (0,)), ((), ())), preferred_element_type=F32).astype(BF16)

    wait(in_b, ab_r.at[1])
    for k in range(len(PEERS_B)):
        total = total + in_b[k]

    quarter = [total] + [pltpu.roll(total, 128 - N_DP * q, 1) for q in range(1, NY)]
    m = jnp.concatenate(quarter, axis=0)
    row = lax.broadcasted_iota(jnp.int32, (N_DP, 128), 0)
    lane = lax.broadcasted_iota(jnp.int32, (N_DP, 128), 1)
    m = jnp.where(lane < N_DP, m, 0.0)
    weight = jnp.ones((N_DP, 1), F32)
    for level in range(5):
        bit = 1 << level
        own = jnp.where(lane == row, m, 0.0)
        mixed = jnp.where(lane == (row ^ bit), m, 0.0)
        down = 1.0 - jnp.sum(mixed, axis=1, keepdims=True) / (2.0 * (jnp.sum(own, axis=1, keepdims=True) + EPS))
        across = 1.0 - jnp.sum(mixed, axis=0, keepdims=True) / (2.0 * (jnp.sum(own, axis=0, keepdims=True) + EPS))
        weight = weight * down
        m = (down * across) * m
        m = m + jnp.where((row & bit) == 0, pltpu.roll(m, N_DP - bit, 0), pltpu.roll(m, bit, 0))
        m = m + jnp.where((lane & bit) == 0, pltpu.roll(m, 128 - bit, 1), pltpu.roll(m, bit, 1))
        m = jnp.where(lane < N_DP, m, 0.0)
    wts[...] = jnp.broadcast_to(weight, (N_DP, 128))

    def combine(step, _):
        at = pl.ds(pl.multiple_of(step * 16, 16), 16)
        value = jnp.zeros((16, WIDE), F32)
        for b in range(N_DP):
            value = value + gv[b, at].astype(F32) * wts[b : b + 1, :]
        out_grad[at, :] = value
        return 0

    lax.fori_loop(0, HEADS // 16, combine, 0, unroll=4)
    whole = (us.at[pl.ds(0, 7)], pack, us.at[pl.ds(0, 7)], ct.at[pl.ds(0, 7)], gv.at[pl.ds(0, 24)], in_a, in_b)
    for kind, ref in enumerate(whole):
        wait(ref, sent.at[kind])


def body(context, cotangent, row_order, out_weight):
    sem = pltpu.SemaphoreType.DMA
    return pl.pallas_call(
        kernel,
        out_shape=(
            jax.ShapeDtypeStruct((HEADS, WIDE), F32),
            jax.ShapeDtypeStruct((ROWS, HEADS), BF16),
        ),
        in_specs=[pl.BlockSpec(memory_space=pl.ANY)] * 4,
        out_specs=[pl.BlockSpec(memory_space=pltpu.VMEM)] * 2,
        scratch_shapes=[
            pltpu.VMEM((NC, NX, SHARD, D), BF16),
            pltpu.VMEM((NZ, NC, NX, SHARD, SLICE), BF16),
            pltpu.VMEM((NZ - 1, SHARD, SLICE), BF16),
            pltpu.VMEM((NZ, 2, HALF, ROWS), BF16),
            pltpu.VMEM((ROWS, HEADS), BF16),
            pltpu.VMEM((1, ROWS), jnp.int32),
            pltpu.VMEM((HEADS, D), BF16),
            pltpu.VMEM((ROWS, ROWS), BF16),
            pltpu.VMEM((NZ, 2, NY, HALF, WIDE), BF16),
            pltpu.VMEM((N_DP, HEADS, WIDE), BF16),
            pltpu.VMEM((2, N_DP * N_DP, 128), F32),
            pltpu.VMEM((8, 128), F32),
            pltpu.VMEM((8, 128), F32),
            pltpu.VMEM((len(PEERS_A), 8, 128), F32),
            pltpu.VMEM((len(PEERS_B), 8, 128), F32),
            pltpu.VMEM((N_DP, 128), F32),
            sem((4,)),
            sem((7,)),
            sem((NZ, 2)),
            sem((NZ,)),
            sem((4,)),
            sem((NZ, 2)),
            sem((NZ, 2)),
            sem((2,)),
        ],
        name="adasum",
        compiler_params=pltpu.CompilerParams(
            collective_id=0, has_side_effects=True, vmem_limit_bytes=int(53.5 * 2**20)
        ),
        cost_estimate=pl.CostEstimate(flops=2_300_000_000, bytes_accessed=4_000_000, transcendentals=0),
    )(context, cotangent, row_order, out_weight)


def solution(mesh):
    in_specs = (P("dp", "tensor"), P(("dp", "tensor"), None), P("dp", None), P("tensor", None))
    out_specs = (P("tensor", "dp"), P("dp", "tensor"))
    return jax.shard_map(body, mesh=mesh, in_specs=in_specs, out_specs=out_specs, check_vma=False)
```

```python
import jax
import jax.numpy as jnp
from jax import lax
from jax.experimental import pallas as pl
from jax.experimental.pallas import tpu as pltpu
from jax.sharding import PartitionSpec as P

EPS = 1e-06
MESH = pl.DeviceIdType.MESH
BF16, F32 = jnp.bfloat16, jnp.float32
NY, NZ, NX, NC = 4, 8, 4, 2
ROWS, SHARD = 512, 64
HEADS, D = 256, 4096
SLICE = D // NZ
WIDE = D // (NY * NZ)
HALF = HEADS // 2
N_DP = NY * NZ
PEERS_A = [(dz, dc) for dz in (4, 3, 5, 2, 6, 1, 7, 0) for dc in (1, 0) if dz or dc]
PEERS_B = [(dy, dx) for dy, dx in sorted(((a, b) for a in range(NY) for b in range(NX)), key=lambda p: -min(p[0], NY - p[0]) - min(p[1], NX - p[1])) if dy or dx]
NEIGHBOURS = [(0, dz, 0, 0) for dz in (2, 6, 1, 7)] + [(dy, 0, 0, 0) for dy in (2, 1, 3)] + [(0, 0, dx, 0) for dx in (2, 1, 3)] + [(0, 0, 0, 1)]


def kernel(
    context, cotangent, row_order, out_weight, out_grad, out_back,
    uf, us, pack, ct, cv, ov, wv, pt, gst, gv, acc, src_a, src_b, in_a, in_b, wts,
    local, sent, us_r, aa_r, uf_r, ct_r, gv_r, ab_r,
):
    dp, tp = lax.axis_index("dp"), lax.axis_index("tensor")
    y, z = lax.div(dp, NZ), lax.rem(dp, NZ)
    x, c = lax.div(tp, NC), lax.rem(tp, NC)

    def device(dy=0, dz=0, dx=0, dc=0):
        return (
            lax.rem(y + dy, NY) * NZ + lax.rem(z + dz, NZ),
            lax.rem(x + dx, NX) * NC + lax.rem(c + dc, NC),
        )

    def send(source, target, kind, recv_sem, where):
        pltpu.make_async_remote_copy(
            src_ref=source, dst_ref=target, send_sem=sent.at[kind], recv_sem=recv_sem,
            device_id=where, device_id_type=MESH,
        ).start()

    def wait(ref, sem):
        pltpu.make_async_copy(ref, ref, sem).wait()

    barrier = pltpu.get_barrier_semaphore()
    for step in NEIGHBOURS:
        pl.semaphore_signal(barrier, inc=1, device_id=device(*step), device_id_type=MESH)

    quarters = [pl.ds(q * SHARD // 4, SHARD // 4) for q in range(4)]
    load_cot = [pltpu.make_async_copy(cotangent.at[q], uf.at[c, x, q], local.at[4 + k]) for k, q in enumerate(quarters)]
    load_ctx = pltpu.make_async_copy(context, cv, local.at[1])
    load_ord = pltpu.make_async_copy(row_order, ov, local.at[2])
    load_w = pltpu.make_async_copy(out_weight, wv, local.at[3])
    for copy in load_cot:
        copy.start()
    load_ctx.start()
    load_ord.start()

    for copy in load_cot:
        copy.wait()
    for d in range(NZ):
        to = lax.rem(z + d, NZ)
        for j in range(NY):
            at = pl.multiple_of((j * NZ + to) * WIDE, WIDE)
            block = uf[c, x, :, pl.ds(at, WIDE)]
            if d == 0:
                us[0, c, x, :, j * WIDE : (j + 1) * WIDE] = block
            else:
                pack[d - 1, :, j * WIDE : (j + 1) * WIDE] = block

    load_ctx.wait()
    load_ord.wait()
    row = lax.broadcasted_iota(jnp.int32, (ROWS, ROWS), 0)
    name = lax.rem(lax.div(row, SHARD), NX) * (NC * SHARD) + lax.div(row, NX * SHARD) * SHARD + lax.rem(row, SHARD)
    pt[...] = (ov[...] == name).astype(F32).astype(BF16)
    mine = lax.dot_general(cv[...], pt[...], (((0,), (1,)), ((), ())), preferred_element_type=F32).astype(BF16)
    ct[0, 0] = mine[:HALF]
    ct[0, 1] = mine[HALF:]
    pl.semaphore_wait(barrier, len(NEIGHBOURS))

    right, left, far, sibling = device(dx=1), device(dx=NX - 1), device(dx=2), device(dc=1)
    xl, xr, xf = lax.rem(x + NX - 1, NX), lax.rem(x + 1, NX), lax.rem(x + 2, NX)
    lo, hi = pl.ds(0, SHARD // 2), pl.ds(SHARD // 2, SHARD // 2)

    def us_own(d):
        mine = us.at[d, c, x]
        for to in (far, right, left):
            send(mine, mine, 0, us_r.at[d, 0], to)

    def us_share(d):
        wait(us.at[d, c, pl.ds(0, 3)], us_r.at[d, 0])
        part = us.at[d, c]
        send(part, part, 0, us_r.at[d, 1], sibling)

    def us_ready(d):
        wait(us.at[d, c], us_r.at[d, 1])

    def aa_send(d):
        send(pack.at[d - 1], us.at[NZ - d, c, x], 1, aa_r.at[NZ - d], device(dz=d))

    def aa_ready(d):
        wait(pack.at[0], aa_r.at[d])

    def uf_own(k):
        for rows, to in ((lo, right), (hi, left)) if k == 0 else ((hi, right), (lo, left)):
            part = uf.at[c, x, rows]
            send(part, part, 2, uf_r.at[k], to)
        if k == 0:
            part = uf.at[c, x]
            send(part, part, 2, uf_r.at[3], sibling)

    def uf_forward():
        wait(uf.at[c, x], uf_r.at[0])
        part = uf.at[c, xl, lo]
        send(part, part, 2, uf_r.at[2], right)
        part = uf.at[c, xr, hi]
        send(part, part, 2, uf_r.at[2], left)

    def uf_share_near():
        wait(uf.at[c, x], uf_r.at[1])
        for at in (xl, xr):
            part = uf.at[c, at]
            send(part, part, 2, uf_r.at[3], sibling)

    def uf_share_far():
        wait(uf.at[c, x], uf_r.at[2])
        part = uf.at[c, xf]
        send(part, part, 2, uf_r.at[3], sibling)

    def ct_send(slot, h, step):
        to = (slot - step) % NZ
        send(ct.at[slot, h], ct.at[to, h], 3, ct_r.at[to, h], device(dz=step % NZ))

    def ct_arrived(d, h):
        wait(ct.at[d, h], ct_r.at[d, h])
        if d in (7, 6) or (d == 5 and h == 0):
            ct_send(d, h, 1)
        if d in (1, 2) or (d == 3 and h == 1):
            ct_send(d, h, -1)

    def replica(d, e=0):
        return lax.rem(y + e, NY) * NZ + lax.rem(z + d, NZ)

    def gv_send(d, h, e):
        target = gv.at[replica(d), pl.ds(h * HALF, HALF)]
        send(gst.at[d, h, lax.rem(y + e, NY)], target, 4, gv_r.at[d, h], device(dy=e))

    def gradient(d, h):
        value = jnp.dot(ct[d, h], us[d].reshape(ROWS, SLICE), preferred_element_type=F32).astype(BF16)
        for j in range(NY):
            gst[d, h, j] = value[:, j * WIDE : (j + 1) * WIDE]
        for e in (2, 1, 3):
            gv_send(d, h, e)
        gv[replica(d), h * HALF : (h + 1) * HALF] = gst[d, h, y]

    def gram_pair(d1, d2, h):
        first = [replica(d1, e) for e in range(NY)]
        second = [replica(d2, e) for e in range(NY)]
        pairs = [(i, j) for i in range(NY) for j in range(NY) if d1 != d2 or i <= j]

        def body(step, sums):
            at = pl.ds(pl.multiple_of(h * HALF + step * 16, 16), 16)
            a = [gv[b, at].astype(F32) for b in first]
            bs = a if d1 == d2 else [gv[b, at].astype(F32) for b in second]
            return tuple(s + a[i] * bs[j] for s, (i, j) in zip(sums, pairs))

        sums = lax.fori_loop(0, HALF // 16, body, tuple(jnp.zeros((16, WIDE), F32) for _ in pairs), unroll=8)
        for s, (i, j) in zip(sums, pairs):
            line = jnp.sum(s, axis=0, keepdims=True)
            zi, yi = lax.rem(z + d1, NZ), lax.rem(y + i, NY)
            zj, yj = lax.rem(z + d2, NZ), lax.rem(y + j, NY)
            acc[h, pl.ds(zi * 128 + yi * N_DP + yj * NZ + zj, 1), :] = line
            acc[h, pl.ds(zj * 128 + yj * N_DP + yi * NZ + zi, 1), :] = line

    done = ([], [])

    def gram_half(d, h):
        wait(gv.at[pl.ds(0, NY - 1), pl.ds(0, HALF)], gv_r.at[d, h])
        done[h].append(d)
        for other in done[h]:
            gram_pair(d, other, h)

    def gram(d):
        for h in range(2):
            gram_half(d, h)

    load_w.start()
    us_own(0)
    for d in (1, 7, 2, 6):
        aa_send(d)
    for h in range(2):
        ct_send(0, h, 1)
        ct_send(0, 1 - h, -1)
    for d in (1, 7):
        aa_ready(d)
        us_own(d)
    us_share(0)
    for d in (2, 6):
        aa_ready(d)
        us_own(d)
    for d in (3, 5, 4):
        aa_send(d)
    us_share(1)
    us_share(7)
    us_ready(0)
    gradient(0, 0)
    gradient(0, 1)
    us_share(2)
    us_share(6)
    for h in range(2):
        ct_arrived(7, h)
        ct_arrived(1, 1 - h)
    us_ready(1)
    us_ready(7)
    for h in range(2):
        gradient(7, h)
        gradient(1, 1 - h)
    for d in (3, 5):
        aa_ready(d)
        us_own(d)
    aa_ready(4)
    us_own(4)
    us_ready(2)
    us_ready(6)
    ct_arrived(6, 0)
    ct_arrived(2, 1)
    gradient(6, 0)
    gradient(2, 1)
    us_share(3)
    us_share(5)
    ct_arrived(6, 1)
    ct_arrived(2, 0)
    gradient(6, 1)
    gradient(2, 0)
    gram(0)
    gram(1)
    us_share(4)
    uf_own(0)
    uf_own(1)
    us_ready(3)
    us_ready(5)
    ct_arrived(5, 0)
    ct_arrived(3, 1)
    gradient(5, 0)
    gradient(3, 1)
    gram(7)
    ct_arrived(5, 1)
    ct_arrived(3, 0)
    gradient(5, 1)
    gradient(3, 0)
    us_ready(4)
    gram(2)
    gram(6)
    ct_arrived(4, 0)
    gradient(4, 0)
    ct_arrived(4, 1)
    gradient(4, 1)
    uf_forward()
    gram_half(5, 0)
    gram_half(3, 1)
    gram_half(5, 1)
    gram_half(3, 0)
    gram_half(4, 0)
    gram_half(4, 1)

    ones = jnp.ones((8, 128), BF16)
    sums = acc[0] + acc[1]
    high = sums.astype(BF16)
    low = (sums - high.astype(F32)).astype(BF16)
    over_lanes = (((1,), (1,)), ((), ()))
    flat = lax.dot_general(ones, high, over_lanes, preferred_element_type=F32) + lax.dot_general(
        ones, low, over_lanes, preferred_element_type=F32
    )
    sub = lax.broadcasted_iota(jnp.int32, (8, 128), 0)
    tile = jnp.zeros((8, 128), F32)
    for i in range(8):
        tile = jnp.where(sub == i, flat[:, i * 128 : (i + 1) * 128], tile)
    src_a[...] = tile
    for k, (dz, dc) in enumerate(PEERS_A):
        send(src_a, in_a.at[k], 5, ab_r.at[0], device(dz=dz, dc=dc))

    uf_share_near()
    wait(in_a, ab_r.at[0])
    total = src_a[...]
    for k in range(len(PEERS_A)):
        total = total + in_a[k]
    src_b[...] = total
    for k, (dy, dx) in enumerate(PEERS_B):
        send(src_b, in_b.at[k], 6, ab_r.at[1], device(dy=dy, dx=dx))
    uf_share_far()
    load_w.wait()
    wait(uf.at[c], uf_r.at[3])
    over_width = (((1,), (1,)), ((), ()))
    parts = []
    for core in range(NC):
        rows = uf[core].reshape(NX * SHARD, D)
        parts.append(
            lax.dot_general(rows, wv[...], over_width, preferred_element_type=F32).astype(BF16)
        )
    gathered = jnp.concatenate(parts, axis=0)
    out_back[...] = lax.dot_general(pt[...], gathered, (((0,), (0,)), ((), ())), preferred_element_type=F32).astype(BF16)

    wait(in_b, ab_r.at[1])
    for k in range(len(PEERS_B)):
        total = total + in_b[k]

    quarter = [total] + [pltpu.roll(total, 128 - N_DP * q, 1) for q in range(1, NY)]
    m = jnp.concatenate(quarter, axis=0)
    row = lax.broadcasted_iota(jnp.int32, (N_DP, 128), 0)
    lane = lax.broadcasted_iota(jnp.int32, (N_DP, 128), 1)
    weight = jnp.ones((N_DP, 1), F32)
    for level in range(5):
        bit = 1 << level
        own = jnp.where(lane == row, m, 0.0)
        mixed = jnp.where(lane == (row ^ bit), m, 0.0)
        down = 1.0 - jnp.sum(mixed, axis=1, keepdims=True) / (2.0 * (jnp.sum(own, axis=1, keepdims=True) + EPS))
        across = 1.0 - jnp.sum(mixed, axis=0, keepdims=True) / (2.0 * (jnp.sum(own, axis=0, keepdims=True) + EPS))
        weight = weight * down
        m = (down * across) * m
        m = m + jnp.where((row & bit) == 0, pltpu.roll(m, N_DP - bit, 0), pltpu.roll(m, bit, 0))
        m = m + jnp.where((lane & bit) == 0, pltpu.roll(m, 128 - bit, 1), pltpu.roll(m, bit, 1))
    wts[...] = jnp.broadcast_to(weight, (N_DP, 128))

    def combine(step, _):
        at = pl.ds(pl.multiple_of(step * 16, 16), 16)
        value = jnp.zeros((16, WIDE), F32)
        for b in range(N_DP):
            value = value + gv[b, at].astype(F32) * wts[b : b + 1, :]
        out_grad[at, :] = value
        return 0

    lax.fori_loop(0, HEADS // 16, combine, 0, unroll=16)
    whole = (us.at[pl.ds(0, 7)], pack, us.at[pl.ds(0, 7)], ct.at[pl.ds(0, 7)], gv.at[pl.ds(0, 24)], in_a, in_b)
    for kind, ref in enumerate(whole):
        wait(ref, sent.at[kind])


def body(context, cotangent, row_order, out_weight):
    sem = pltpu.SemaphoreType.DMA
    return pl.pallas_call(
        kernel,
        out_shape=(
            jax.ShapeDtypeStruct((HEADS, WIDE), F32),
            jax.ShapeDtypeStruct((ROWS, HEADS), BF16),
        ),
        in_specs=[pl.BlockSpec(memory_space=pl.ANY)] * 4,
        out_specs=[pl.BlockSpec(memory_space=pltpu.VMEM)] * 2,
        scratch_shapes=[
            pltpu.VMEM((NC, NX, SHARD, D), BF16),
            pltpu.VMEM((NZ, NC, NX, SHARD, SLICE), BF16),
            pltpu.VMEM((NZ - 1, SHARD, SLICE), BF16),
            pltpu.VMEM((NZ, 2, HALF, ROWS), BF16),
            pltpu.VMEM((ROWS, HEADS), BF16),
            pltpu.VMEM((1, ROWS), jnp.int32),
            pltpu.VMEM((HEADS, D), BF16),
            pltpu.VMEM((ROWS, ROWS), BF16),
            pltpu.VMEM((NZ, 2, NY, HALF, WIDE), BF16),
            pltpu.VMEM((N_DP, HEADS, WIDE), BF16),
            pltpu.VMEM((2, N_DP * N_DP, 128), F32),
            pltpu.VMEM((8, 128), F32),
            pltpu.VMEM((8, 128), F32),
            pltpu.VMEM((len(PEERS_A), 8, 128), F32),
            pltpu.VMEM((len(PEERS_B), 8, 128), F32),
            pltpu.VMEM((N_DP, 128), F32),
            sem((8,)),
            sem((7,)),
            sem((NZ, 2)),
            sem((NZ,)),
            sem((4,)),
            sem((NZ, 2)),
            sem((NZ, 2)),
            sem((2,)),
        ],
        name="adasum",
        compiler_params=pltpu.CompilerParams(
            collective_id=0, has_side_effects=True, vmem_limit_bytes=int(53.5 * 2**20)
        ),
        cost_estimate=pl.CostEstimate(flops=2_300_000_000, bytes_accessed=4_000_000, transcendentals=0),
    )(context, cotangent, row_order, out_weight)


def solution(mesh):
    in_specs = (P("dp", "tensor"), P(("dp", "tensor"), None), P("dp", None), P("tensor", None))
    out_specs = (P("tensor", "dp"), P("dp", "tensor"))
    return jax.shard_map(body, mesh=mesh, in_specs=in_specs, out_specs=out_specs, check_vma=False)
```
